128 devices in a mesh: cluster: 4 (over z_lo, core), group: 32 (over y, z_hi, x).
Axes of the slice: x: 4, y: 4, z: 4 (z_hi: 2, z_lo: 2; z = z_hi * 2 + z_lo), core: 2. Of those that a mesh axis runs over, the one named last changes fastest.
Arguments:
- embeddings: float32 [49152, 512], P(('cluster', 'group')), may hold values from -220 to 220
- destinations: int32 [49152, 1], P(('cluster', 'group')), may hold values from 0 to 127; in each aligned block of 384 rows (0 to 383, 384 to 767, ...) at most 6 rows name the same one
Outputs:
- nearest: float32 [49152], P(('cluster', 'group'))
The draws below stay inside these ranges and needn't reach their ends.
Inputs may be any that keep to these rules, and one draw needn't show every extreme that they name: `destinations`: among the rows of one device no destination is named more than 6 times, a bound that some block reaches.
All inputs are finite; a program needn't handle non-finite values.
Results may differ from the reference program's by a relative error of at most 0.005.
Values may be sent and summed in bfloat16 or wider, within the bound.
A program may use at most 64 MiB of HBM per device.

```python
import math
import jax
import jax.numpy as jnp
import numpy as np
from jax import lax

E = 512
R_DEV = 384
ROWS = 49152
CAP = 6
N_GROUP = 32
DEVICES = 128


def draw_embeddings(key, part):
    key = jax.random.fold_in(key, 7)
    keys = jax.random.split(key, 4)
    noise = jnp.clip(jax.random.normal(keys[0], (ROWS, E), jnp.float32), -6.0, 6.0)
    shared = jax.random.randint(keys[1], (ROWS,), 0, ROWS // 4)
    common = jnp.clip(jax.random.normal(keys[2], (ROWS // 4, E), jnp.float32), -6.0, 6.0)
    weight = jax.random.uniform(keys[3], (ROWS, 1), jnp.float32, 0.0, 2.0)
    values = noise + weight * common[shared]
    return values.astype(jnp.float32)


def routed_block(rng, own, number, rows, number_of, top, bound, skew):
    ranking = jax.random.permutation(rng, number_of)
    crowded, usual = load_shares(number_of, rows * top, bound, skew, True), load_shares(number_of, rows * top, bound, skew, False)
    places = jnp.arange(number_of)

    def named(tallies, offset_by):
        used = int((tallies > 0).sum())
        fixed = max(1, used // 4)
        moved = fixed + (places - fixed + offset_by * (used - fixed)) % max(1, number_of - fixed)
        return jnp.zeros((number_of,), jnp.int32).at[ranking[jnp.where(places < fixed, places, moved)]].set(jnp.asarray(tallies, jnp.int32))

    tallies = jnp.where(number % 4 == 0, named(crowded, number // 4), named(usual, number - number // 4 - 1))
    mixed = jax.random.permutation(jax.random.fold_in(own, 3), number_of)
    giver, taker = mixed[0:number_of // 2 * 2:2], mixed[1:number_of // 2 * 2:2]
    slack = jnp.minimum(tallies[giver] - 1, bound - tallies[taker]) // 2
    slack = jnp.where((giver == ranking[0]) | (taker == ranking[0]) | (tallies[taker] == 0), 0, jnp.maximum(slack, 0))
    moved = jax.random.randint(jax.random.fold_in(own, 4), (number_of // 2,), 0, 1 << 20) % (slack + 1)
    tallies = tallies.at[giver].add(-moved).at[taker].add(moved)
    items = jnp.searchsorted(jnp.cumsum(tallies), jnp.arange(rows * top), side="right").astype(jnp.int32)
    grid = items.reshape(top, rows).T
    grid = grid[jax.random.permutation(jax.random.fold_in(own, 1), rows)]
    offset_by = jax.random.randint(jax.random.fold_in(own, 2), (rows, 1), 0, top)
    return jnp.take_along_axis(grid, (jnp.arange(top)[None, :] + offset_by) % top, axis=1)


def load_shares(number_of, total, bound, lean, full):
    weights = [(1 << 20) // math.isqrt(rank ** lean) + 1 for rank in range(1, number_of + 1)]
    largest = bound if full else min(bound, max(-(-total // number_of), total * weights[0] // sum(weights)))
    least = 1 if total - largest >= number_of - 1 else 0
    holding, spare = [largest] + [least] * (number_of - 1), total - largest - least * (number_of - 1)
    while spare > 0:
        free = [i for i in range(1, number_of) if holding[i] < largest] or [i for i in range(1, number_of) if holding[i] < bound]
        mass, left = sum([weights[i] for i in free]), spare
        for i in free:
            more = min(bound - holding[i], max(1, left * weights[i] // mass), spare)
            holding[i] = holding[i] + more
            spare = spare - more
    return np.array(holding)


def setup_inputs(seed: int = 0) -> dict:
    splits = jax.random.split(jax.random.key(seed), 3)
    embeddings = draw_embeddings(jax.random.fold_in(splits[2], 71), 0)
    destinations_keys = jax.random.split(jax.random.fold_in(splits[1], 1), ROWS // R_DEV)
    destinations_turns = jax.random.permutation(jax.random.fold_in(splits[1], 3), ROWS // R_DEV)
    destinations = jax.vmap(lambda own, number: routed_block(jax.random.fold_in(splits[1], 2), own, number, R_DEV, DEVICES, 1, CAP, 2))(destinations_keys, destinations_turns).reshape((ROWS, 1))
    return {"embeddings": embeddings, "destinations": destinations}


def reference(embeddings, destinations):
    sums = lax.optimization_barrier(jnp.sum(embeddings * embeddings, axis=1, keepdims=True))
    unit = (embeddings * lax.rsqrt(sums + 1e-06)).astype(jnp.bfloat16).astype(jnp.float32)
    cluster = (destinations[:, 0] // N_GROUP).astype(jnp.int32)
    blocks = ROWS // R_DEV
    unit_blocks = unit.reshape(blocks, R_DEV, E)
    cluster_blocks = cluster.reshape(blocks, R_DEV)
    starts = (jnp.arange(blocks) * R_DEV).astype(jnp.int32)
    every_index = jnp.arange(ROWS).astype(jnp.int32)

    def one_block(packed):
        rows, labels, start = packed
        scores = jnp.dot(rows, unit.T, precision=lax.Precision.HIGHEST, preferred_element_type=jnp.float32)
        own_index = start + jnp.arange(R_DEV).astype(jnp.int32)
        match = (labels[:, None] == cluster[None, :]) & (own_index[:, None] != every_index[None, :])
        return lax.optimization_barrier(jnp.max(jnp.where(match, scores, jnp.float32(-2.0)), axis=1))
    nearest = lax.map(one_block, (unit_blocks, cluster_blocks, starts))
    return nearest.reshape(ROWS)
```

```python
import functools

import jax
import jax.numpy as jnp
from jax import lax
from jax.experimental import pallas as pl
from jax.experimental.pallas import tpu as pltpu
from jax.sharding import PartitionSpec as P

MESH = pl.DeviceIdType.MESH
HALF = 384
WIDTH = 512
TILE = 16
UNITS = ((1, 0, 0), (3, 0, 0), (0, 1, 0), (0, 3, 0), (0, 0, 1), (0, 0, 3))
SLOTS = 13
OFFSETS = ((0, 0, 0), (0, 1, 0), (0, 3, 1), (0, 0, 3), (1, 0, 0), (0, 2, 1), (0, 3, 0), (2, 0, 0), (3, 0, 3), (2, 0, 3), (0, 2, 0), (0, 0, 1), (0, 1, 1))
PARTS = ((0, 128), (128, 128), (256, 144))
ACTS = (
    ("D", 0), ("S", 0, 4, 0, 0), ("S", 0, 1, 1, 2), ("S", 0, 6, 1, 3), ("S", 0, 11, 0, 4), ("S", 0, 3, 2, 5),
    ("S", 0, 4, 1, 0), ("S", 0, 1, 2, 2), ("S", 0, 6, 2, 3), ("S", 0, 11, 2, 4), ("S", 0, 3, 1, 5), ("self", 0),
    ("X", 0), ("self", 1), ("S", 0, 4, 2, 0), ("S", 0, 1, 0, 2), ("S", 0, 3, 0, 5), ("S", 0, 11, 1, 4), ("R", 4, 0),
    ("S", 4, 7, 0, 0), ("R", 1, 1), ("R", 6, 1), ("S", 6, 2, 1, 4), ("R", 11, 0), ("S", 11, 2, 0, 3), ("R", 3, 2),
    ("S", 3, 8, 2, 1), ("S", 11, 12, 0, 2), ("S", 1, 12, 1, 4), ("R", 4, 1), ("S", 4, 7, 1, 0), ("R", 1, 2),
    ("R", 6, 2), ("R", 11, 2), ("S", 11, 12, 2, 2), ("S", 11, 2, 2, 3), ("R", 3, 1), ("S", 3, 8, 1, 1), ("R", 8, 2),
    ("R", 4, 2), ("S", 4, 7, 2, 0), ("D", 4), ("R", 1, 0), ("D", 1), ("R", 2, 0), ("S", 2, 5, 0, 3),
    ("S", 2, 6, 0, 5), ("R", 11, 1), ("D", 11), ("R", 3, 0), ("S", 3, 8, 0, 1), ("D", 3), ("G", 4, (0,)),
    ("G", 1, (0,)), ("G", 3, (0,)), ("S", 8, 9, 2, 1), ("S", 1, 10, 2, 2), ("S", 6, 10, 1, 3), ("X", 4),
    ("G", 11, (4,)), ("R", 8, 1), ("S", 8, 9, 1, 1), ("X", 3), ("X", 1), ("G", 4, (3, 1)), ("R", 7, 0),
    ("S", 7, 9, 0, 5), ("R", 12, 0), ("R", 2, 2), ("R", 2, 1), ("S", 2, 5, 1, 3), ("D", 2), ("G", 2, (0, 4)),
    ("G", 2, (1, 3)), ("R", 6, 0), ("D", 6), ("R", 8, 0), ("D", 8), ("G", 8, (4, 1)), ("R", 7, 1), ("R", 12, 2),
    ("S", 12, 5, 2, 2), ("R", 5, 0), ("S", 5, 10, 0, 5), ("R", 12, 1), ("D", 12), ("X", 2), ("X", 11),
    ("G", 8, (2, 11)), ("G", 6, (1, 4)), ("R", 9, 2), ("X", 8), ("G", 12, (4, 8)), ("R", 9, 0), ("R", 7, 2),
    ("D", 7), ("R", 10, 2), ("R", 10, 1), ("G", 7, (0, 1)), ("F", 0), ("X", 12), ("G", 7, (2, 12)), ("F", 12),
    ("R", 9, 1), ("G", 9, (2, 11)), ("F", 2), ("R", 10, 0), ("R", 5, 2), ("R", 5, 1), ("D", 5), ("G", 5, (4, 3)),
    ("G", 10, (4, 8)), ("F", 4), ("G", 3, (1,)), ("F", 1), ("G", 11, (3,)), ("F", 3), ("F", 11), ("X", 6),
    ("G", 8, (6,)), ("F", 6), ("G", 5, (8,)), ("F", 8), ("X", 5), ("G", 7, (5,)), ("G", 9, (5,)), ("F", 9),
    ("F", 5), ("X", 7), ("G", 10, (7,)), ("F", 10), ("F", 7),
)


def place():
    cluster = lax.axis_index("cluster")
    group = lax.axis_index("group")
    core = lax.rem(cluster, 2)
    z = cluster // 2 + 2 * lax.rem(group // 4, 2)
    return (lax.rem(group, 4), group // 8, z), core


def device(chip, offset, core):
    x, y, z = (lax.rem(a + b, 4) for a, b in zip(chip, offset))
    return (lax.rem(z, 2) * 2 + core, (y * 2 + z // 2) * 4 + x)


def back(offset):
    return tuple((4 - v) % 4 for v in offset)


def kernel(emb_ref, dest_ref, out_ref, blk, labc, racc, cacc, res,
           ici_send, ici_recv, d2d_send, d2d_recv, res_send, res_recv):
    chip, core = place()
    other = 1 - core
    barrier = pltpu.get_barrier_semaphore()
    for unit in UNITS:
        pl.semaphore_signal(barrier, inc=1, device_id=device(chip, unit, core), device_id_type=MESH)
    sibling = device(chip, (0, 0, 0), other)
    pl.semaphore_signal(barrier, inc=1, device_id=sibling, device_id_type=MESH)

    values = emb_ref[...]
    sums = jnp.sum(values * values, axis=1, keepdims=True)
    blk[0, core, 0:HALF, :] = (values * lax.rsqrt(sums + 1e-06)).astype(jnp.bfloat16)
    label = (dest_ref[...] // 32).astype(jnp.float32)
    tile = jnp.concatenate(
        [jnp.broadcast_to(label, (TILE, HALF)), jnp.zeros((TILE, WIDTH - HALF), jnp.float32)], axis=1)
    blk[0, core, HALF:HALF + TILE, :] = tile.astype(jnp.bfloat16)
    pl.semaphore_wait(barrier, len(UNITS) + 1)

    sends = []

    def ici(src, dst, part, e):
        first, count = PARTS[part]
        rows = pl.ds(first, count)
        return pltpu.make_async_remote_copy(
            src_ref=blk.at[src, core, rows], dst_ref=blk.at[dst, core, rows],
            send_sem=ici_send.at[dst, part], recv_sem=ici_recv.at[dst, part],
            device_id=device(chip, back(UNITS[e]), core), device_id_type=MESH)

    def d2d(slot, half):
        return pltpu.make_async_remote_copy(
            src_ref=blk.at[slot, half], dst_ref=blk.at[slot, half],
            send_sem=d2d_send.at[slot], recv_sem=d2d_recv.at[slot],
            device_id=sibling, device_id_type=MESH)

    def result(slot, half, sender):
        return pltpu.make_async_remote_copy(
            src_ref=cacc.at[slot, half], dst_ref=res.at[slot, sender],
            send_sem=res_send.at[slot, half], recv_sem=res_recv.at[slot, sender],
            device_id=device(chip, OFFSETS[slot], half), device_id_type=MESH)

    def labels(slot, half):
        return blk[slot, half, HALF:HALF + TILE, :].astype(jnp.float32)[0:8, 0:HALF]

    def column_labels(slot):
        row = labels(slot, core)
        labc[slot] = jnp.concatenate([row] * 16, axis=0).T

    have_labc, have_racc, have_cacc = set(), set(), set()

    def prepare(slot):
        if slot not in have_labc:
            have_labc.add(slot)
            column_labels(slot)

    def masked(scores, own, row):
        count = scores.shape[0] // 8
        match = own.reshape(count, 8, 128) == row[None]
        return jnp.where(match, scores.reshape(count, 8, 128), jnp.float32(-2.0))

    def dot(lhs, rhs):
        return lax.dot_general(lhs, rhs, (((1,), (1,)), ((), ())), preferred_element_type=jnp.float32)

    def own_block(which):
        prepare(0)
        half = core if which == 0 else other
        scores = dot(blk[0, core, 0:HALF, :], blk[0, half, 0:HALF, :])
        row = labels(0, half)
        own = labc[0]
        best = racc[0] if 0 in have_racc else jnp.full((HALF, 128), -2.0, jnp.float32)
        for q in range(0, HALF, 128):
            t = masked(scores[:, q:q + 128], own, row[:, q:q + 128]).reshape(HALF, 128)
            if which == 0:
                i = lax.broadcasted_iota(jnp.int32, (HALF, 128), 0)
                j = lax.broadcasted_iota(jnp.int32, (HALF, 128), 1) + q
                t = jnp.where(i == j, jnp.float32(-2.0), t)
            best = jnp.maximum(best, t)
        racc[0] = best
        have_racc.add(0)

    def pairs(slot, others):
        prepare(slot)
        lhs = blk[slot, core, 0:HALF, :]
        own = labc[slot]
        best = racc[slot] if slot in have_racc else None
        for mate in others:
            scores = dot(lhs, blk[mate, :, 0:HALF, :].reshape(2 * HALF, WIDTH))
            for half in range(2):
                row = labels(mate, half)
                for q in range(0, HALF, 128):
                    at = half * HALF + q
                    t = masked(scores[:, at:at + 128], own, row[:, q:q + 128])
                    top = jnp.max(t, axis=0)
                    if mate in have_cacc:
                        top = jnp.maximum(top, cacc[mate, half, :, q:q + 128])
                    cacc[mate, half, :, q:q + 128] = top
                    t = t.reshape(HALF, 128)
                    best = t if best is None else jnp.maximum(best, t)
            have_cacc.add(mate)
        racc[slot] = best
        have_racc.add(slot)

    def finish(slot):
        if slot in have_racc:
            best = jnp.max(racc[slot].T.reshape(16, 8, HALF), axis=0)
            if slot in have_cacc:
                best = jnp.maximum(best, cacc[slot, core])
            cacc[slot, core] = best
        if slot == 0:
            copy = result(0, other, 1)
            copy.start()
            sends.append(copy)
        elif slot in have_cacc:
            for half in range(2):
                copy = result(slot, half, core)
                copy.start()
                sends.append(copy)
        else:
            copy = result(slot, core, core)
            copy.start()
            sends.append(copy)

    for act in ACTS:
        kind = act[0]
        if kind == "S":
            copy = ici(act[1], act[2], act[3], act[4])
            copy.start()
            sends.append(copy)
        elif kind == "R":
            ici(act[1], act[1], act[2], 0).wait_recv()
        elif kind == "D":
            copy = d2d(act[1], core)
            copy.start()
            sends.append(copy)
        elif kind == "X":
            d2d(act[1], other).wait_recv()
        elif kind == "self":
            own_block(act[1])
        elif kind == "G":
            pairs(act[1], act[2])
        else:
            finish(act[1])

    result(0, other, 1).wait_recv()
    best = jnp.maximum(cacc[0, core], res[0, 1])
    for slot in range(1, SLOTS):
        if slot in have_cacc:
            for sender in range(2):
                result(slot, core, sender).wait_recv()
                best = jnp.maximum(best, res[slot, sender])
        else:
            result(slot, core, core).wait_recv()
            best = jnp.maximum(best, res[slot, core])
    out_ref[...] = jnp.max(best, axis=0, keepdims=True)
    for copy in sends:
        copy.wait_send()


def on_device(embeddings, destinations):
    nearest = pl.pallas_call(
        kernel,
        out_shape=jax.ShapeDtypeStruct((1, HALF), jnp.float32),
        in_specs=[pl.BlockSpec(memory_space=pltpu.VMEM)] * 2,
        out_specs=pl.BlockSpec(memory_space=pltpu.VMEM),
        scratch_shapes=[
            pltpu.VMEM((SLOTS, 2, HALF + TILE, WIDTH), jnp.bfloat16),
            pltpu.VMEM((SLOTS, HALF, 128), jnp.float32),
            pltpu.VMEM((SLOTS, HALF, 128), jnp.float32),
            pltpu.VMEM((SLOTS, 2, 8, HALF), jnp.float32),
            pltpu.VMEM((SLOTS, 2, 8, HALF), jnp.float32),
            pltpu.SemaphoreType.DMA((SLOTS, len(PARTS))),
            pltpu.SemaphoreType.DMA((SLOTS, len(PARTS))),
            pltpu.SemaphoreType.DMA((SLOTS,)),
            pltpu.SemaphoreType.DMA((SLOTS,)),
            pltpu.SemaphoreType.DMA((SLOTS, 2)),
            pltpu.SemaphoreType.DMA((SLOTS, 2)),
        ],
        compiler_params=pltpu.CompilerParams(
            collective_id=0, has_side_effects=True, vmem_limit_bytes=48 * 2**20),
    )(embeddings, destinations.reshape(1, HALF))
    return nearest.reshape(HALF)


def solution(mesh):
    spec = P(("cluster", "group"), None)
    return jax.shard_map(
        on_device, mesh=mesh, in_specs=(spec, spec), out_specs=P(("cluster", "group")), check_vma=False
    )
```

```python
import functools

import jax
import jax.numpy as jnp
from jax import lax
from jax.experimental import pallas as pl
from jax.experimental.pallas import tpu as pltpu
from jax.sharding import PartitionSpec as P

MESH = pl.DeviceIdType.MESH
HALF = 384
WIDTH = 512
TILE = 16
UNITS = ((1, 0, 0), (3, 0, 0), (0, 1, 0), (0, 3, 0), (0, 0, 1), (0, 0, 3))
SLOTS = 13
OFFSETS = ((0, 0, 0), (0, 3, 3), (1, 0, 0), (0, 1, 0), (0, 0, 1), (0, 0, 2), (0, 3, 0), (3, 1, 0), (0, 3, 2), (3, 0, 0), (1, 1, 0), (2, 0, 0), (2, 1, 0))
PARTS = ((0, 128), (128, 128), (256, 144))
ACTS = (
    ("S", 0, 2, 0, 0), ("S", 0, 9, 1, 1), ("S", 0, 3, 1, 2), ("S", 0, 6, 1, 3), ("S", 0, 4, 1, 4),
    ("S", 0, 2, 2, 0), ("S", 0, 9, 0, 1), ("S", 0, 3, 0, 2), ("S", 0, 6, 2, 3), ("S", 0, 4, 2, 4), ("D", 0),
    ("self", 0), ("X", 0), ("self", 1), ("S", 0, 9, 2, 1), ("S", 0, 3, 2, 2), ("S", 0, 6, 0, 3), ("R", 2, 0),
    ("R", 9, 1), ("R", 3, 1), ("S", 3, 10, 1, 0), ("R", 6, 1), ("S", 6, 1, 1, 5), ("S", 0, 4, 0, 4), ("R", 4, 1),
    ("S", 4, 5, 1, 4), ("R", 2, 2), ("S", 2, 10, 2, 2), ("R", 9, 0), ("R", 3, 0), ("S", 3, 10, 0, 0),
    ("S", 3, 7, 0, 1), ("S", 9, 7, 1, 2), ("R", 6, 2), ("S", 6, 1, 2, 5), ("R", 4, 2), ("S", 4, 5, 2, 4),
    ("R", 1, 1), ("R", 10, 1), ("S", 10, 2, 1, 3), ("S", 10, 12, 1, 0), ("R", 9, 2), ("D", 9), ("R", 3, 2),
    ("S", 3, 7, 2, 1), ("D", 3), ("R", 6, 0), ("S", 6, 1, 0, 5), ("D", 6), ("R", 4, 0), ("S", 4, 5, 0, 4), ("D", 4),
    ("G", 6, (0,)), ("G", 9, (0,)), ("G", 4, (0,)), ("X", 9), ("G", 3, (9,)), ("G", 6, (9,)), ("G", 4, (9,)),
    ("R", 1, 2), ("S", 1, 8, 2, 5), ("R", 10, 0), ("R", 7, 0), ("S", 7, 12, 0, 1), ("R", 10, 2),
    ("S", 10, 12, 2, 0), ("S", 2, 11, 2, 0), ("S", 9, 11, 0, 1), ("D", 10), ("R", 5, 1), ("S", 5, 8, 1, 3),
    ("X", 6), ("X", 3), ("X", 4), ("G", 3, (6,)), ("G", 4, (3, 6)), ("G", 10, (6, 9, 4)), ("R", 2, 1),
    ("G", 2, (4, 9)), ("R", 1, 0), ("S", 1, 8, 0, 5), ("D", 1), ("R", 12, 1), ("S", 12, 11, 1, 3), ("R", 7, 2),
    ("R", 7, 1), ("D", 7), ("R", 5, 2), ("X", 10), ("G", 1, (3, 9, 4, 10)), ("G", 7, (4,)), ("X", 1),
    ("G", 2, (1,)), ("G", 7, (1,)), ("F", 2), ("R", 8, 1), ("R", 8, 2), ("R", 12, 2), ("R", 12, 0), ("D", 12),
    ("R", 5, 0), ("D", 5), ("X", 7), ("G", 5, (7, 10, 0, 9)), ("G", 12, (4, 1, 6)), ("F", 7), ("F", 0), ("F", 9),
    ("F", 6), ("R", 8, 0), ("R", 11, 1), ("R", 11, 2), ("R", 11, 0), ("X", 12), ("X", 5), ("G", 5, (12,)),
    ("G", 8, (3, 12, 10)), ("G", 11, (5, 4, 1)), ("F", 3), ("F", 12), ("F", 8), ("F", 10), ("F", 5), ("F", 4),
    ("F", 11), ("F", 1),
)


def place():
    cluster = lax.axis_index("cluster")
    group = lax.axis_index("group")
    core = lax.rem(cluster, 2)
    z = cluster // 2 + 2 * lax.rem(group // 4, 2)
    return (lax.rem(group, 4), group // 8, z), core


def device(chip, offset, core):
    x, y, z = (lax.rem(a + b, 4) for a, b in zip(chip, offset))
    return (lax.rem(z, 2) * 2 + core, (y * 2 + z // 2) * 4 + x)


def back(offset):
    return tuple((4 - v) % 4 for v in offset)


def kernel(emb_any, dest_any, out_ref, emb_ref, dest_ref, load_sem, blk, labc, racc, cacc, part, res,
           ici_send, ici_recv, d2d_send, d2d_recv, res_send, res_recv):
    chip, core = place()
    other = 1 - core
    loads = [pltpu.make_async_copy(emb_any, emb_ref, load_sem.at[0]),
             pltpu.make_async_copy(dest_any, dest_ref, load_sem.at[1])]
    for load in loads:
        load.start()
    barrier = pltpu.get_barrier_semaphore()
    for unit in UNITS:
        pl.semaphore_signal(barrier, inc=1, device_id=device(chip, unit, core), device_id_type=MESH)
    sibling = device(chip, (0, 0, 0), other)
    pl.semaphore_signal(barrier, inc=1, device_id=sibling, device_id_type=MESH)

    for load in loads:
        load.wait()
    values = emb_ref[...]
    sums = jnp.sum(values * values, axis=1, keepdims=True)
    blk[0, core, 0:HALF, :] = (values * lax.rsqrt(sums + 1e-06)).astype(jnp.bfloat16)
    label = (dest_ref[...] // 32).astype(jnp.float32)
    tile = jnp.concatenate(
        [jnp.broadcast_to(label, (TILE, HALF)), jnp.zeros((TILE, WIDTH - HALF), jnp.float32)], axis=1)
    blk[0, core, HALF:HALF + TILE, :] = tile.astype(jnp.bfloat16)
    pl.semaphore_wait(barrier, len(UNITS) + 1)

    sends = []

    def ici(src, dst, part, e):
        first, count = PARTS[part]
        rows = pl.ds(first, count)
        return pltpu.make_async_remote_copy(
            src_ref=blk.at[src, core, rows], dst_ref=blk.at[dst, core, rows],
            send_sem=ici_send.at[dst, part], recv_sem=ici_recv.at[dst, part],
            device_id=device(chip, back(UNITS[e]), core), device_id_type=MESH)

    def d2d(slot, half):
        return pltpu.make_async_remote_copy(
            src_ref=blk.at[slot, half], dst_ref=blk.at[slot, half],
            send_sem=d2d_send.at[slot], recv_sem=d2d_recv.at[slot],
            device_id=sibling, device_id_type=MESH)

    def result(slot, half, sender):
        return pltpu.make_async_remote_copy(
            src_ref=part.at[slot, half], dst_ref=res.at[slot, sender],
            send_sem=res_send.at[slot, half], recv_sem=res_recv.at[slot, sender],
            device_id=device(chip, OFFSETS[slot], half), device_id_type=MESH)

    def labels(slot, half):
        return blk[slot, half, HALF:HALF + TILE, :].astype(jnp.float32)[0:8, 0:HALF]

    def column_labels(slot):
        row = labels(slot, core)
        labc[slot] = jnp.concatenate([row] * 16, axis=0).T

    have_labc, have_racc, have_cacc = set(), set(), set()

    def prepare(slot):
        if slot not in have_labc:
            have_labc.add(slot)
            column_labels(slot)

    def masked(scores, own, row):
        count = scores.shape[0] // 8
        match = own.reshape(count, 8, 128) == row[None]
        return jnp.where(match, scores.reshape(count, 8, 128), jnp.float32(-2.0))

    def dot(lhs, rhs):
        return lax.dot_general(lhs, rhs, (((1,), (1,)), ((), ())), preferred_element_type=jnp.float32)

    def own_block(which):
        prepare(0)
        half = core if which == 0 else other
        scores = dot(blk[0, core, 0:HALF, :], blk[0, half, 0:HALF, :])
        row = labels(0, half)
        own = labc[0]
        best = racc[0] if 0 in have_racc else jnp.full((HALF, 128), -2.0, jnp.float32)
        for q in range(0, HALF, 128):
            t = masked(scores[:, q:q + 128], own, row[:, q:q + 128]).reshape(HALF, 128)
            if which == 0:
                i = lax.broadcasted_iota(jnp.int32, (HALF, 128), 0)
                j = lax.broadcasted_iota(jnp.int32, (HALF, 128), 1) + q
                t = jnp.where(i == j, jnp.float32(-2.0), t)
            best = jnp.maximum(best, t)
        racc[0] = best
        have_racc.add(0)

    def pairs(slot, others):
        prepare(slot)
        lhs = blk[slot, core, 0:HALF, :]
        own = labc[slot]
        best = racc[slot] if slot in have_racc else None
        for mate in others:
            scores = dot(lhs, blk[mate, :, 0:HALF, :].reshape(2 * HALF, WIDTH))
            for half in range(2):
                row = labels(mate, half)
                for q in range(0, HALF, 128):
                    at = half * HALF + q
                    t = masked(scores[:, at:at + 128], own, row[:, q:q + 128])
                    top = jnp.max(t, axis=0)
                    if mate in have_cacc:
                        top = jnp.maximum(top, cacc[mate, half, :, q:q + 128])
                    cacc[mate, half, :, q:q + 128] = top
                    t = t.reshape(HALF, 128)
                    best = t if best is None else jnp.maximum(best, t)
            have_cacc.add(mate)
        racc[slot] = best
        have_racc.add(slot)

    def finish(slot):
        if slot in have_racc:
            best = jnp.max(racc[slot].T.reshape(16, 8, HALF), axis=0)
            if slot in have_cacc:
                best = jnp.maximum(best, cacc[slot, core])
            part[slot, core] = jnp.max(best, axis=0, keepdims=True)
        if slot in have_cacc:
            part[slot, other] = jnp.max(cacc[slot, other], axis=0, keepdims=True)
            if slot not in have_racc:
                part[slot, core] = jnp.max(cacc[slot, core], axis=0, keepdims=True)
        if slot == 0:
            copy = result(0, other, 1)
            copy.start()
            sends.append(copy)
        elif slot in have_cacc:
            for half in range(2):
                copy = result(slot, half, core)
                copy.start()
                sends.append(copy)
        else:
            copy = result(slot, core, core)
            copy.start()
            sends.append(copy)

    for act in ACTS:
        kind = act[0]
        if kind == "S":
            copy = ici(act[1], act[2], act[3], act[4])
            copy.start()
            sends.append(copy)
        elif kind == "R":
            ici(act[1], act[1], act[2], 0).wait_recv()
        elif kind == "D":
            copy = d2d(act[1], core)
            copy.start()
            sends.append(copy)
        elif kind == "X":
            d2d(act[1], other).wait_recv()
        elif kind == "self":
            own_block(act[1])
        elif kind == "G":
            pairs(act[1], act[2])
        else:
            finish(act[1])

    result(0, other, 1).wait_recv()
    best = jnp.maximum(part[0, core], res[0, 1])
    for slot in range(1, SLOTS):
        if slot in have_cacc:
            for sender in range(2):
                result(slot, core, sender).wait_recv()
                best = jnp.maximum(best, res[slot, sender])
        else:
            result(slot, core, core).wait_recv()
            best = jnp.maximum(best, res[slot, core])
    out_ref[...] = best.reshape(HALF)
    for copy in sends:
        copy.wait_send()


def on_device(embeddings, destinations):
    nearest = pl.pallas_call(
        kernel,
        out_shape=jax.ShapeDtypeStruct((HALF,), jnp.float32),
        in_specs=[pl.BlockSpec(memory_space=pl.ANY)] * 2,
        out_specs=pl.BlockSpec(memory_space=pltpu.VMEM),
        scratch_shapes=[
            pltpu.VMEM((HALF, WIDTH), jnp.float32),
            pltpu.VMEM((1, HALF), jnp.int32),
            pltpu.SemaphoreType.DMA((2,)),
            pltpu.VMEM((SLOTS, 2, HALF + TILE, WIDTH), jnp.bfloat16),
            pltpu.VMEM((SLOTS, HALF, 128), jnp.float32),
            pltpu.VMEM((SLOTS, HALF, 128), jnp.float32),
            pltpu.VMEM((SLOTS, 2, 8, HALF), jnp.float32),
            pltpu.VMEM((SLOTS, 2, 1, HALF), jnp.float32),
            pltpu.VMEM((SLOTS, 2, 1, HALF), jnp.float32),
            pltpu.SemaphoreType.DMA((SLOTS, len(PARTS))),
            pltpu.SemaphoreType.DMA((SLOTS, len(PARTS))),
            pltpu.SemaphoreType.DMA((SLOTS,)),
            pltpu.SemaphoreType.DMA((SLOTS,)),
            pltpu.SemaphoreType.DMA((SLOTS, 2)),
            pltpu.SemaphoreType.DMA((SLOTS, 2)),
        ],
        compiler_params=pltpu.CompilerParams(
            collective_id=0, has_side_effects=True, vmem_limit_bytes=63 * 2**20),
    )(embeddings, destinations.reshape(1, HALF))
    return nearest


def solution(mesh):
    spec = P(("cluster", "group"), None)
    return jax.shard_map(
        on_device, mesh=mesh, in_specs=(spec, spec), out_specs=P(("cluster", "group")), check_vma=False
    )
```

```python
import functools

import jax
import jax.numpy as jnp
from jax import lax
from jax.experimental import pallas as pl
from jax.experimental.pallas import tpu as pltpu
from jax.sharding import PartitionSpec as P

MESH = pl.DeviceIdType.MESH
HALF = 384
WIDTH = 512
TILE = 16
UNITS = ((1, 0, 0), (3, 0, 0), (0, 1, 0), (0, 3, 0), (0, 0, 1), (0, 0, 3))
SLOTS = 13
OFFSETS = ((0, 0, 0), (0, 1, 0), (1, 1, 0), (0, 3, 0), (1, 0, 0), (3, 0, 0), (3, 0, 3), (0, 2, 0), (3, 0, 2), (0, 0, 1), (1, 2, 0), (1, 3, 0), (0, 0, 2))
PARTS = ((0, 128), (128, 128), (256, 144))
ACTS = (
    ("S", 0, 4, 0, 0), ("S", 0, 5, 0, 1), ("S", 0, 1, 2, 2), ("S", 0, 3, 2, 3), ("S", 0, 9, 0, 4), ("D", 0),
    ("self", 0), ("X", 0), ("self", 1), ("S", 0, 4, 1, 0), ("S", 0, 5, 1, 1), ("S", 0, 1, 1, 2), ("S", 0, 3, 1, 3),
    ("S", 0, 9, 2, 4), ("S", 0, 5, 2, 1), ("S", 0, 3, 0, 3), ("S", 0, 9, 1, 4), ("R", 4, 0), ("S", 4, 2, 0, 2),
    ("R", 5, 0), ("S", 5, 6, 0, 5), ("R", 1, 2), ("S", 1, 2, 2, 0), ("R", 3, 2), ("R", 9, 0), ("S", 0, 4, 2, 0),
    ("R", 4, 1), ("S", 4, 2, 1, 2), ("S", 4, 11, 1, 3), ("R", 5, 1), ("S", 5, 6, 1, 5), ("R", 1, 1), ("R", 3, 1),
    ("R", 9, 2), ("S", 9, 12, 2, 4), ("S", 3, 11, 2, 0), ("S", 4, 11, 0, 3), ("R", 6, 0), ("R", 2, 2), ("R", 5, 2),
    ("S", 5, 6, 2, 5), ("D", 5), ("R", 2, 0), ("S", 2, 1, 0, 1), ("S", 2, 10, 0, 2), ("R", 3, 0), ("D", 3),
    ("R", 9, 1), ("S", 9, 12, 1, 4), ("D", 9), ("G", 9, (0,)), ("G", 3, (0,)), ("G", 5, (0,)), ("F", 0),
    ("S", 6, 8, 0, 5), ("S", 2, 10, 2, 2), ("S", 9, 12, 0, 4), ("X", 3), ("X", 5), ("G", 9, (3, 5)), ("G", 5, (3,)),
    ("R", 6, 1), ("R", 4, 2), ("D", 4), ("R", 2, 1), ("D", 2), ("R", 11, 1), ("S", 11, 10, 1, 3), ("R", 12, 2),
    ("S", 12, 8, 2, 1), ("X", 9), ("G", 2, (5, 3, 9)), ("G", 4, (9, 5, 3)), ("S", 6, 8, 1, 5), ("S", 1, 7, 1, 2),
    ("S", 3, 7, 2, 3), ("R", 6, 2), ("D", 6), ("R", 1, 0), ("X", 2), ("X", 4), ("G", 6, (2, 3, 4)),
    ("G", 1, (3, 9)), ("R", 11, 2), ("R", 10, 0), ("S", 10, 7, 0, 1), ("R", 11, 0), ("D", 11), ("R", 12, 1),
    ("X", 6), ("G", 11, (9,)), ("G", 1, (6,)), ("G", 9, (6,)), ("F", 1), ("R", 8, 0), ("R", 8, 2), ("R", 10, 2),
    ("R", 10, 1), ("D", 10), ("R", 12, 0), ("D", 12), ("X", 11), ("G", 12, (3, 11, 2)), ("G", 10, (9, 6, 5)),
    ("G", 6, (11,)), ("F", 11), ("F", 3), ("R", 8, 1), ("X", 10), ("X", 12), ("G", 8, (2, 10, 4, 5)),
    ("G", 10, (12,)), ("F", 10), ("F", 8), ("F", 2), ("F", 4), ("F", 5), ("R", 7, 1), ("R", 7, 2), ("R", 7, 0),
    ("G", 7, (9, 6, 12)), ("F", 6), ("F", 7), ("F", 12), ("F", 9),
)


def place():
    cluster = lax.axis_index("cluster")
    group = lax.axis_index("group")
    core = lax.rem(cluster, 2)
    z = cluster // 2 + 2 * lax.rem(group // 4, 2)
    return (lax.rem(group, 4), group // 8, z), core


def device(chip, offset, core):
    x, y, z = (lax.rem(a + b, 4) for a, b in zip(chip, offset))
    return (lax.rem(z, 2) * 2 + core, (y * 2 + z // 2) * 4 + x)


def back(offset):
    return tuple((4 - v) % 4 for v in offset)


def kernel(emb_any, dest_any, out_ref, emb_ref, dest_ref, load_sem, blk, labc, racc, cacc, part, res,
           ici_send, ici_recv, d2d_send, d2d_recv, res_send, res_recv):
    chip, core = place()
    other = 1 - core
    barrier = pltpu.get_barrier_semaphore()
    for unit in UNITS:
        pl.semaphore_signal(barrier, inc=1, device_id=device(chip, unit, core), device_id_type=MESH)
    sibling = device(chip, (0, 0, 0), other)
    pl.semaphore_signal(barrier, inc=1, device_id=sibling, device_id_type=MESH)

    loads = [pltpu.make_async_copy(emb_any, emb_ref, load_sem.at[0]),
             pltpu.make_async_copy(dest_any, dest_ref, load_sem.at[1])]
    for load in loads:
        load.start()
    for load in loads:
        load.wait()
    values = emb_ref[...]
    sums = jnp.sum(values * values, axis=1, keepdims=True)
    blk[0, core, 0:HALF, :] = (values * lax.rsqrt(sums + 1e-06)).astype(jnp.bfloat16)
    label = (dest_ref[...] // 32).astype(jnp.float32)
    tile = jnp.concatenate(
        [jnp.broadcast_to(label, (TILE, HALF)), jnp.zeros((TILE, WIDTH - HALF), jnp.float32)], axis=1)
    blk[0, core, HALF:HALF + TILE, :] = tile.astype(jnp.bfloat16)
    pl.semaphore_wait(barrier, len(UNITS) + 1)

    def ici(src, dst, piece, e):
        first, count = PARTS[piece]
        rows = pl.ds(first, count)
        return pltpu.make_async_remote_copy(
            src_ref=blk.at[src, core, rows], dst_ref=blk.at[dst, core, rows],
            send_sem=ici_send.at[0], recv_sem=ici_recv.at[dst, piece],
            device_id=device(chip, back(UNITS[e]), core), device_id_type=MESH)

    def d2d(slot, half):
        return pltpu.make_async_remote_copy(
            src_ref=blk.at[slot, half], dst_ref=blk.at[slot, half],
            send_sem=d2d_send.at[0], recv_sem=d2d_recv.at[slot],
            device_id=sibling, device_id_type=MESH)

    def result(slot, half, sender):
        return pltpu.make_async_remote_copy(
            src_ref=part.at[2 * slot + half], dst_ref=res.at[2 * slot + sender],
            send_sem=res_send.at[0], recv_sem=res_recv.at[0],
            device_id=device(chip, OFFSETS[slot], half), device_id_type=MESH)

    def results(count):
        return pltpu.make_async_remote_copy(
            src_ref=part.at[pl.ds(0, count)], dst_ref=res.at[pl.ds(0, count)],
            send_sem=res_send.at[0], recv_sem=res_recv.at[0],
            device_id=sibling, device_id_type=MESH)

    def sent(first, count, sem):
        rows = blk.at[pl.ds(first, count), core]
        return pltpu.make_async_remote_copy(
            src_ref=rows, dst_ref=rows, send_sem=sem, recv_sem=ici_recv.at[0, 0],
            device_id=sibling, device_id_type=MESH)

    def labels(slot, half):
        return blk[slot, half, HALF:HALF + TILE, :].astype(jnp.float32)[0:8, 0:HALF]

    def column_labels(slot):
        row = labels(slot, core)
        labc[slot] = jnp.concatenate([row] * 16, axis=0).T

    have_labc, have_racc, have_cacc = set(), set(), set()

    def prepare(slot):
        if slot not in have_labc:
            have_labc.add(slot)
            column_labels(slot)

    def masked(scores, own, row):
        count = scores.shape[0] // 8
        match = own.reshape(count, 8, 128) == row[None]
        return jnp.where(match, scores.reshape(count, 8, 128), jnp.float32(-2.0))

    def dot(lhs, rhs):
        return lax.dot_general(lhs, rhs, (((1,), (1,)), ((), ())), preferred_element_type=jnp.float32)

    def own_block(which):
        prepare(0)
        half = core if which == 0 else other
        scores = dot(blk[0, core, 0:HALF, :], blk[0, half, 0:HALF, :])
        row = labels(0, half)
        own = labc[0]
        best = racc[0] if 0 in have_racc else jnp.full((HALF, 128), -2.0, jnp.float32)
        for q in range(0, HALF, 128):
            t = masked(scores[:, q:q + 128], own, row[:, q:q + 128]).reshape(HALF, 128)
            if which == 0:
                i = lax.broadcasted_iota(jnp.int32, (HALF, 128), 0)
                j = lax.broadcasted_iota(jnp.int32, (HALF, 128), 1) + q
                t = jnp.where(i == j, jnp.float32(-2.0), t)
            best = jnp.maximum(best, t)
        racc[0] = best
        have_racc.add(0)

    def pairs(slot, others):
        prepare(slot)
        lhs = blk[slot, core, 0:HALF, :]
        own = labc[slot]
        best = racc[slot] if slot in have_racc else None
        for mate in others:
            scores = dot(lhs, blk[mate, :, 0:HALF, :].reshape(2 * HALF, WIDTH))
            for half in range(2):
                row = labels(mate, half)
                for q in range(0, HALF, 128):
                    at = half * HALF + q
                    t = masked(scores[:, at:at + 128], own, row[:, q:q + 128])
                    top = jnp.max(t, axis=0)
                    if mate in have_cacc:
                        top = jnp.maximum(top, cacc[mate, half, :, q:q + 128])
                    cacc[mate, half, :, q:q + 128] = top
                    t = t.reshape(HALF, 128)
                    best = t if best is None else jnp.maximum(best, t)
            have_cacc.add(mate)
        racc[slot] = best
        have_racc.add(slot)

    def finish(slot):
        if slot in have_racc:
            best = jnp.max(racc[slot].T.reshape(16, 8, HALF), axis=0)
            if slot in have_cacc:
                best = jnp.maximum(best, cacc[slot, core])
            part[2 * slot + core] = jnp.max(best, axis=0, keepdims=True)
        if slot in have_cacc:
            part[2 * slot + other] = jnp.max(cacc[slot, other], axis=0, keepdims=True)
            if slot not in have_racc:
                part[2 * slot + core] = jnp.max(cacc[slot, core], axis=0, keepdims=True)

    def send_back(slot):
        halves = (other,) if slot == 0 else (0, 1) if slot in have_cacc else (core,)
        for half in halves:
            result(slot, half, 1 if slot == 0 else core).start()

    finished = []
    for act in ACTS + (("",),):
        kind = act[0]
        if kind != "F":
            for slot in finished:
                send_back(slot)
            finished = []
        if kind == "S":
            ici(act[1], act[2], act[3], act[4]).start()
        elif kind == "R":
            ici(act[1], act[1], act[2], 0).wait_recv()
        elif kind == "D":
            d2d(act[1], core).start()
        elif kind == "X":
            d2d(act[1], other).wait_recv()
        elif kind == "self":
            own_block(act[1])
        elif kind == "G":
            pairs(act[1], act[2])
        elif kind == "F":
            finish(act[1])
            finished.append(act[1])

    sent(1, SLOTS - 1, ici_send.at[0]).wait_send()
    sent(0, sum(act[0] == "D" for act in ACTS), d2d_send.at[0]).wait_send()
    count = 1 + sum(2 if slot in have_cacc else 1 for slot in range(1, SLOTS))
    results(count).wait_send()
    results(count).wait_recv()
    best = jnp.maximum(part[core], res[1])
    for slot in range(1, SLOTS):
        if slot in have_cacc:
            best = jnp.maximum(best, jnp.maximum(res[2 * slot], res[2 * slot + 1]))
        else:
            best = jnp.maximum(best, res[2 * slot + core])
    out_ref[...] = best.reshape(HALF)


def on_device(embeddings, destinations):
    nearest = pl.pallas_call(
        kernel,
        out_shape=jax.ShapeDtypeStruct((HALF,), jnp.float32),
        in_specs=[pl.BlockSpec(memory_space=pl.ANY)] * 2,
        out_specs=pl.BlockSpec(memory_space=pltpu.VMEM),
        scratch_shapes=[
            pltpu.VMEM((HALF, WIDTH), jnp.float32),
            pltpu.VMEM((1, HALF), jnp.int32),
            pltpu.SemaphoreType.DMA((2,)),
            pltpu.VMEM((SLOTS, 2, HALF + TILE, WIDTH), jnp.bfloat16),
            pltpu.VMEM((SLOTS, HALF, 128), jnp.float32),
            pltpu.VMEM((SLOTS, HALF, 128), jnp.float32),
            pltpu.VMEM((SLOTS, 2, 8, HALF), jnp.float32),
            pltpu.VMEM((2 * SLOTS, 1, HALF), jnp.float32),
            pltpu.VMEM((2 * SLOTS, 1, HALF), jnp.float32),
            pltpu.SemaphoreType.DMA((1,)),
            pltpu.SemaphoreType.DMA((SLOTS, len(PARTS))),
            pltpu.SemaphoreType.DMA((1,)),
            pltpu.SemaphoreType.DMA((SLOTS,)),
            pltpu.SemaphoreType.DMA((1,)),
            pltpu.SemaphoreType.DMA((1,)),
        ],
        compiler_params=pltpu.CompilerParams(
            collective_id=0, has_side_effects=True, vmem_limit_bytes=63 * 2**20),
    )(embeddings, destinations.reshape(1, HALF))
    return nearest


def solution(mesh):
    spec = P(("cluster", "group"), None)
    return jax.shard_map(
        on_device, mesh=mesh, in_specs=(spec, spec), out_specs=P(("cluster", "group")), check_vma=False
    )
```

```python
import functools

import jax
import jax.numpy as jnp
from jax import lax
from jax.experimental import pallas as pl
from jax.experimental.pallas import tpu as pltpu
from jax.sharding import PartitionSpec as P

MESH = pl.DeviceIdType.MESH
HALF = 384
WIDTH = 512
TILE = 16
UNITS = ((1, 0, 0), (3, 0, 0), (0, 1, 0), (0, 3, 0), (0, 0, 1), (0, 0, 3))
SLOTS = 13
OFFSETS = ((0, 0, 0), (0, 1, 0), (1, 1, 0), (0, 3, 0), (1, 0, 0), (3, 0, 0), (3, 0, 3), (0, 2, 0), (3, 0, 2), (0, 0, 1), (1, 2, 0), (1, 3, 0), (0, 0, 2))
PARTS = ((0, 128), (128, 128), (256, 144))
ACTS = (
    ("S", 0, 4, 0, 0), ("S", 0, 5, 0, 1), ("S", 0, 1, 2, 2), ("S", 0, 3, 2, 3), ("S", 0, 9, 0, 4), ("D", 0),
    ("self", 0), ("X", 0), ("self", 1), ("S", 0, 4, 1, 0), ("S", 0, 5, 1, 1), ("S", 0, 1, 1, 2), ("S", 0, 3, 1, 3),
    ("S", 0, 9, 2, 4), ("S", 0, 5, 2, 1), ("S", 0, 3, 0, 3), ("S", 0, 9, 1, 4), ("R", 4, 0), ("S", 4, 2, 0, 2),
    ("R", 5, 0), ("S", 5, 6, 0, 5), ("R", 1, 2), ("S", 1, 2, 2, 0), ("R", 3, 2), ("R", 9, 0), ("S", 0, 4, 2, 0),
    ("R", 4, 1), ("S", 4, 2, 1, 2), ("S", 4, 11, 1, 3), ("R", 5, 1), ("S", 5, 6, 1, 5), ("R", 1, 1), ("R", 3, 1),
    ("R", 9, 2), ("S", 9, 12, 2, 4), ("S", 3, 11, 2, 0), ("S", 4, 11, 0, 3), ("R", 6, 0), ("R", 2, 2), ("R", 5, 2),
    ("S", 5, 6, 2, 5), ("D", 5), ("R", 2, 0), ("S", 2, 1, 0, 1), ("S", 2, 10, 0, 2), ("R", 3, 0), ("D", 3),
    ("R", 9, 1), ("S", 9, 12, 1, 4), ("D", 9), ("G", 5, (0,)), ("G", 3, (0,)), ("G", 9, (0,)), ("X", 5),
    ("G", 3, (5,)), ("S", 6, 8, 0, 5), ("X", 3), ("X", 9), ("G", 9, (3,)), ("G", 5, (9,)), ("S", 2, 10, 2, 2),
    ("S", 9, 12, 0, 4), ("R", 6, 1), ("R", 4, 2), ("D", 4), ("R", 2, 1), ("D", 2), ("R", 11, 1),
    ("S", 11, 10, 1, 3), ("R", 12, 2), ("S", 12, 8, 2, 1), ("G", 2, (5, 3, 9)), ("G", 4, (5, 3, 9)),
    ("S", 6, 8, 1, 5), ("S", 1, 7, 1, 2), ("S", 3, 7, 2, 3), ("R", 6, 2), ("D", 6), ("R", 1, 0), ("X", 4), ("X", 2),
    ("G", 6, (3, 4, 9, 2)), ("G", 1, (9, 3)), ("R", 11, 2), ("R", 10, 0), ("S", 10, 7, 0, 1), ("R", 11, 0),
    ("D", 11), ("R", 12, 1), ("X", 6), ("G", 11, (6, 9)), ("G", 1, (6,)), ("F", 1), ("R", 8, 0), ("R", 8, 2),
    ("R", 10, 2), ("R", 10, 1), ("D", 10), ("R", 12, 0), ("D", 12), ("X", 11), ("G", 12, (0, 11, 2, 3)),
    ("G", 10, (9, 5, 6)), ("F", 0), ("F", 11), ("F", 3), ("F", 5), ("R", 8, 1), ("R", 7, 1), ("R", 7, 2), ("X", 10),
    ("G", 12, (10,)), ("G", 8, (10, 4, 2)), ("F", 10), ("F", 4), ("F", 8), ("F", 2), ("R", 7, 0), ("X", 12),
    ("G", 7, (6, 12, 9)), ("F", 6), ("F", 12), ("F", 7), ("F", 9),
)


def place():
    cluster = lax.axis_index("cluster")
    group = lax.axis_index("group")
    core = lax.rem(cluster, 2)
    z = cluster // 2 + 2 * lax.rem(group // 4, 2)
    return (lax.rem(group, 4), group // 8, z), core


def device(chip, offset, core):
    x, y, z = (lax.rem(a + b, 4) for a, b in zip(chip, offset))
    return (lax.rem(z, 2) * 2 + core, (y * 2 + z // 2) * 4 + x)


def back(offset):
    return tuple((4 - v) % 4 for v in offset)


def kernel(emb_any, dest_any, out_ref, emb_ref, dest_ref, load_sem, blk, labc, racc, cacc, part, res,
           ici_send, ici_recv, d2d_send, d2d_recv, res_send, res_recv):
    chip, core = place()
    other = 1 - core
    barrier = pltpu.get_barrier_semaphore()
    for unit in UNITS:
        pl.semaphore_signal(barrier, inc=1, device_id=device(chip, unit, core), device_id_type=MESH)
    sibling = device(chip, (0, 0, 0), other)
    pl.semaphore_signal(barrier, inc=1, device_id=sibling, device_id_type=MESH)

    loads = [pltpu.make_async_copy(emb_any, emb_ref, load_sem.at[0]),
             pltpu.make_async_copy(dest_any, dest_ref, load_sem.at[1])]
    for load in loads:
        load.start()
    for load in loads:
        load.wait()
    values = emb_ref[...]
    sums = jnp.sum(values * values, axis=1, keepdims=True)
    blk[0, core, 0:HALF, :] = (values * lax.rsqrt(sums + 1e-06)).astype(jnp.bfloat16)
    label = (dest_ref[...] // 32).astype(jnp.float32)
    tile = jnp.concatenate(
        [jnp.broadcast_to(label, (TILE, HALF)), jnp.zeros((TILE, WIDTH - HALF), jnp.float32)], axis=1)
    blk[0, core, HALF:HALF + TILE, :] = tile.astype(jnp.bfloat16)
    pl.semaphore_wait(barrier, len(UNITS) + 1)

    def ici(src, dst, piece, e):
        first, count = PARTS[piece]
        rows = pl.ds(first, count)
        return pltpu.make_async_remote_copy(
            src_ref=blk.at[src, core, rows], dst_ref=blk.at[dst, core, rows],
            send_sem=ici_send.at[0], recv_sem=ici_recv.at[dst, piece],
            device_id=device(chip, back(UNITS[e]), core), device_id_type=MESH)

    def d2d(slot, half):
        return pltpu.make_async_remote_copy(
            src_ref=blk.at[slot, half], dst_ref=blk.at[slot, half],
            send_sem=d2d_send.at[0], recv_sem=d2d_recv.at[slot],
            device_id=sibling, device_id_type=MESH)

    def result(slot, half, sender):
        return pltpu.make_async_remote_copy(
            src_ref=part.at[2 * slot + half], dst_ref=res.at[2 * slot + sender],
            send_sem=res_send.at[0], recv_sem=res_recv.at[0],
            device_id=device(chip, OFFSETS[slot], half), device_id_type=MESH)

    def results(count):
        return pltpu.make_async_remote_copy(
            src_ref=part.at[pl.ds(0, count)], dst_ref=res.at[pl.ds(0, count)],
            send_sem=res_send.at[0], recv_sem=res_recv.at[0],
            device_id=sibling, device_id_type=MESH)

    def sent(first, count, sem):
        rows = blk.at[pl.ds(first, count), core]
        return pltpu.make_async_remote_copy(
            src_ref=rows, dst_ref=rows, send_sem=sem, recv_sem=ici_recv.at[0, 0],
            device_id=sibling, device_id_type=MESH)

    def labels(slot, half):
        return blk[slot, half, HALF:HALF + TILE, :].astype(jnp.float32)[0:8, 0:HALF]

    def column_labels(slot):
        row = labels(slot, core)
        labc[slot] = jnp.concatenate([row] * 16, axis=0).T

    have_labc, have_racc, have_cacc = set(), set(), set()

    def prepare(slot):
        if slot not in have_labc:
            have_labc.add(slot)
            column_labels(slot)

    def masked(scores, own, row):
        count = scores.shape[0] // 8
        match = own.reshape(count, 8, 128) == row[None]
        return jnp.where(match, scores.reshape(count, 8, 128), jnp.float32(-2.0))

    def dot(lhs, rhs):
        return lax.dot_general(lhs, rhs, (((1,), (1,)), ((), ())), preferred_element_type=jnp.float32)

    def own_block(which):
        prepare(0)
        half = core if which == 0 else other
        scores = dot(blk[0, core, 0:HALF, :], blk[0, half, 0:HALF, :])
        row = labels(0, half)
        own = labc[0]
        best = racc[0] if 0 in have_racc else jnp.full((HALF, 128), -2.0, jnp.float32)
        for q in range(0, HALF, 128):
            t = masked(scores[:, q:q + 128], own, row[:, q:q + 128]).reshape(HALF, 128)
            if which == 0:
                i = lax.broadcasted_iota(jnp.int32, (HALF, 128), 0)
                j = lax.broadcasted_iota(jnp.int32, (HALF, 128), 1) + q
                t = jnp.where(i == j, jnp.float32(-2.0), t)
            best = jnp.maximum(best, t)
        racc[0] = best
        have_racc.add(0)

    def pairs(slot, others):
        prepare(slot)
        lhs = blk[slot, core, 0:HALF, :]
        own = labc[slot]
        best = racc[slot] if slot in have_racc else None
        for mate in others:
            scores = dot(lhs, blk[mate, :, 0:HALF, :].reshape(2 * HALF, WIDTH))
            for half in range(2):
                row = labels(mate, half)
                for q in range(0, HALF, 128):
                    at = half * HALF + q
                    t = masked(scores[:, at:at + 128], own, row[:, q:q + 128])
                    top = jnp.max(t, axis=0)
                    if mate in have_cacc:
                        top = jnp.maximum(top, cacc[mate, half, :, q:q + 128])
                    cacc[mate, half, :, q:q + 128] = top
                    t = t.reshape(HALF, 128)
                    best = t if best is None else jnp.maximum(best, t)
            have_cacc.add(mate)
        racc[slot] = best
        have_racc.add(slot)

    def finish(slot):
        if slot in have_racc:
            best = jnp.max(racc[slot].T.reshape(16, 8, HALF), axis=0)
            if slot in have_cacc:
                best = jnp.maximum(best, cacc[slot, core])
            part[2 * slot + core] = jnp.max(best, axis=0, keepdims=True)
        if slot in have_cacc:
            part[2 * slot + other] = jnp.max(cacc[slot, other], axis=0, keepdims=True)
            if slot not in have_racc:
                part[2 * slot + core] = jnp.max(cacc[slot, core], axis=0, keepdims=True)

    def send_back(slot):
        halves = (other,) if slot == 0 else (0, 1) if slot in have_cacc else (core,)
        for half in halves:
            result(slot, half, 1 if slot == 0 else core).start()

    finished = []
    for act in ACTS + (("",),):
        kind = act[0]
        if kind != "F":
            for slot in finished:
                send_back(slot)
            finished = []
        if kind == "S":
            ici(act[1], act[2], act[3], act[4]).start()
        elif kind == "R":
            ici(act[1], act[1], act[2], 0).wait_recv()
        elif kind == "D":
            d2d(act[1], core).start()
        elif kind == "X":
            d2d(act[1], other).wait_recv()
        elif kind == "self":
            own_block(act[1])
        elif kind == "G":
            pairs(act[1], act[2])
        elif kind == "F":
            finish(act[1])
            finished.append(act[1])

    sent(1, SLOTS - 1, ici_send.at[0]).wait_send()
    sent(0, sum(act[0] == "D" for act in ACTS), d2d_send.at[0]).wait_send()
    count = 1 + sum(2 if slot in have_cacc else 1 for slot in range(1, SLOTS))
    results(count).wait_send()
    results(count).wait_recv()
    best = jnp.maximum(part[core], res[1])
    for slot in range(1, SLOTS):
        if slot in have_cacc:
            best = jnp.maximum(best, jnp.maximum(res[2 * slot], res[2 * slot + 1]))
        else:
            best = jnp.maximum(best, res[2 * slot + core])
    out_ref[...] = best.reshape(HALF)


def on_device(embeddings, destinations):
    nearest = pl.pallas_call(
        kernel,
        out_shape=jax.ShapeDtypeStruct((HALF,), jnp.float32),
        in_specs=[pl.BlockSpec(memory_space=pl.ANY)] * 2,
        out_specs=pl.BlockSpec(memory_space=pltpu.VMEM),
        scratch_shapes=[
            pltpu.VMEM((HALF, WIDTH), jnp.float32),
            pltpu.VMEM((1, HALF), jnp.int32),
            pltpu.SemaphoreType.DMA((2,)),
            pltpu.VMEM((SLOTS, 2, HALF + TILE, WIDTH), jnp.bfloat16),
            pltpu.VMEM((SLOTS, HALF, 128), jnp.float32),
            pltpu.VMEM((SLOTS, HALF, 128), jnp.float32),
            pltpu.VMEM((SLOTS, 2, 8, HALF), jnp.float32),
            pltpu.VMEM((2 * SLOTS, 1, HALF), jnp.float32),
            pltpu.VMEM((2 * SLOTS, 1, HALF), jnp.float32),
            pltpu.SemaphoreType.DMA((1,)),
            pltpu.SemaphoreType.DMA((SLOTS, len(PARTS))),
            pltpu.SemaphoreType.DMA((1,)),
            pltpu.SemaphoreType.DMA((SLOTS,)),
            pltpu.SemaphoreType.DMA((1,)),
            pltpu.SemaphoreType.DMA((1,)),
        ],
        compiler_params=pltpu.CompilerParams(
            collective_id=0, has_side_effects=True, vmem_limit_bytes=63 * 2**20),
    )(embeddings, destinations.reshape(1, HALF))
    return nearest


def solution(mesh):
    spec = P(("cluster", "group"), None)
    return jax.shard_map(
        on_device, mesh=mesh, in_specs=(spec, spec), out_specs=P(("cluster", "group")), check_vma=False
    )
```

```python
import functools

import jax
import jax.numpy as jnp
from jax import lax
from jax.experimental import pallas as pl
from jax.experimental.pallas import tpu as pltpu
from jax.sharding import PartitionSpec as P

MESH = pl.DeviceIdType.MESH
HALF = 384
WIDTH = 512
TILE = 16
UNITS = ((1, 0, 0), (3, 0, 0), (0, 1, 0), (0, 3, 0), (0, 0, 1), (0, 0, 3))
SLOTS = 13
OFFSETS = ((0, 0, 0), (0, 1, 0), (1, 1, 0), (0, 3, 0), (1, 0, 0), (3, 0, 0), (3, 0, 3), (0, 2, 0), (3, 0, 2), (0, 0, 1), (1, 2, 0), (1, 3, 0), (0, 0, 2))
PARTS = ((0, 128), (128, 128), (256, 144))
ACTS = (
    ("S", 0, 4, 0, 0), ("S", 0, 5, 0, 1), ("S", 0, 1, 2, 2), ("S", 0, 3, 2, 3), ("S", 0, 9, 0, 4), ("D", 0),
    ("self", 0), ("X", 0), ("self", 1), ("S", 0, 4, 1, 0), ("S", 0, 5, 1, 1), ("S", 0, 1, 1, 2), ("S", 0, 3, 1, 3),
    ("S", 0, 9, 2, 4), ("S", 0, 5, 2, 1), ("S", 0, 3, 0, 3), ("S", 0, 9, 1, 4), ("R", 4, 0), ("S", 4, 2, 0, 2),
    ("R", 5, 0), ("S", 5, 6, 0, 5), ("R", 1, 2), ("S", 1, 2, 2, 0), ("R", 3, 2), ("R", 9, 0), ("S", 0, 4, 2, 0),
    ("R", 4, 1), ("S", 4, 2, 1, 2), ("S", 4, 11, 1, 3), ("R", 5, 1), ("S", 5, 6, 1, 5), ("R", 1, 1), ("R", 3, 1),
    ("R", 9, 2), ("S", 9, 12, 2, 4), ("S", 3, 11, 2, 0), ("S", 4, 11, 0, 3), ("R", 6, 0), ("R", 2, 2), ("R", 5, 2),
    ("S", 5, 6, 2, 5), ("D", 5), ("R", 2, 0), ("S", 2, 1, 0, 1), ("S", 2, 10, 0, 2), ("R", 3, 0), ("D", 3),
    ("R", 9, 1), ("S", 9, 12, 1, 4), ("D", 9), ("G", 5, (0,)), ("G", 3, (0,)), ("G", 9, (0,)), ("X", 5),
    ("G", 3, (5,)), ("S", 6, 8, 0, 5), ("X", 3), ("X", 9), ("G", 9, (3,)), ("G", 5, (9,)), ("S", 2, 10, 2, 2),
    ("S", 9, 12, 0, 4), ("R", 6, 1), ("R", 4, 2), ("D", 4), ("R", 2, 1), ("D", 2), ("R", 11, 1),
    ("S", 11, 10, 1, 3), ("R", 12, 2), ("S", 12, 8, 2, 1), ("G", 2, (5, 3, 9)), ("G", 4, (5, 3, 9)),
    ("S", 6, 8, 1, 5), ("S", 1, 7, 1, 2), ("S", 3, 7, 2, 3), ("R", 6, 2), ("D", 6), ("R", 1, 0), ("X", 4), ("X", 2),
    ("G", 6, (3, 4, 9, 2)), ("G", 1, (9, 3)), ("R", 11, 2), ("R", 10, 0), ("S", 10, 7, 0, 1), ("R", 11, 0),
    ("D", 11), ("R", 12, 1), ("X", 6), ("G", 11, (6, 9)), ("G", 1, (6,)), ("F", 1), ("R", 8, 0), ("R", 8, 2),
    ("R", 10, 2), ("R", 10, 1), ("D", 10), ("R", 12, 0), ("D", 12), ("X", 11), ("G", 12, (0, 11, 2, 3)),
    ("G", 10, (9, 5, 6)), ("F", 0), ("F", 11), ("F", 3), ("F", 5), ("R", 8, 1), ("R", 7, 1), ("R", 7, 2), ("X", 10),
    ("G", 12, (10,)), ("G", 8, (10, 4, 2)), ("F", 10), ("F", 4), ("F", 8), ("F", 2), ("R", 7, 0), ("X", 12),
    ("G", 7, (6, 12, 9)), ("F", 6), ("F", 12), ("F", 7), ("F", 9),
)


def place():
    cluster = lax.axis_index("cluster")
    group = lax.axis_index("group")
    core = lax.rem(cluster, 2)
    z = cluster // 2 + 2 * lax.rem(group // 4, 2)
    return (lax.rem(group, 4), group // 8, z), core


def device(chip, offset, core):
    x, y, z = (lax.rem(a + b, 4) for a, b in zip(chip, offset))
    return (lax.rem(z, 2) * 2 + core, (y * 2 + z // 2) * 4 + x)


def back(offset):
    return tuple((4 - v) % 4 for v in offset)


def hops(slot):
    return sum(min(v, 4 - v) for v in OFFSETS[slot])


def kernel(emb_any, dest_any, out_ref, emb_ref, dest_ref, load_sem, blk, labc, racc, cacc, part, res,
           ici_send, ici_recv, d2d_send, d2d_recv, res_send, res_recv):
    chip, core = place()
    other = 1 - core
    barrier = pltpu.get_barrier_semaphore()
    for unit in UNITS:
        pl.semaphore_signal(barrier, inc=1, device_id=device(chip, unit, core), device_id_type=MESH)
    sibling = device(chip, (0, 0, 0), other)
    pl.semaphore_signal(barrier, inc=1, device_id=sibling, device_id_type=MESH)

    loads = [pltpu.make_async_copy(emb_any, emb_ref, load_sem.at[0]),
             pltpu.make_async_copy(dest_any, dest_ref, load_sem.at[1])]
    for load in loads:
        load.start()
    for load in loads:
        load.wait()
    values = emb_ref[...]
    sums = jnp.sum(values * values, axis=1, keepdims=True)
    blk[0, core, 0:HALF, :] = (values * lax.rsqrt(sums + 1e-06)).astype(jnp.bfloat16)
    label = (dest_ref[...] // 32).astype(jnp.float32)
    tile = jnp.concatenate(
        [jnp.broadcast_to(label, (TILE, HALF)), jnp.zeros((TILE, WIDTH - HALF), jnp.float32)], axis=1)
    blk[0, core, HALF:HALF + TILE, :] = tile.astype(jnp.bfloat16)
    pl.semaphore_wait(barrier, len(UNITS) + 1)

    def ici(src, dst, piece, e):
        first, count = PARTS[piece]
        rows = pl.ds(first, count)
        return pltpu.make_async_remote_copy(
            src_ref=blk.at[src, core, rows], dst_ref=blk.at[dst, core, rows],
            send_sem=ici_send.at[0], recv_sem=ici_recv.at[dst, piece],
            device_id=device(chip, back(UNITS[e]), core), device_id_type=MESH)

    def d2d(slot, half):
        return pltpu.make_async_remote_copy(
            src_ref=blk.at[slot, half], dst_ref=blk.at[slot, half],
            send_sem=d2d_send.at[0], recv_sem=d2d_recv.at[slot],
            device_id=sibling, device_id_type=MESH)

    def result(slot, half, sender):
        return pltpu.make_async_remote_copy(
            src_ref=part.at[2 * slot + half], dst_ref=res.at[2 * slot + sender],
            send_sem=res_send.at[0], recv_sem=res_recv.at[0],
            device_id=device(chip, OFFSETS[slot], half), device_id_type=MESH)

    def results(count):
        return pltpu.make_async_remote_copy(
            src_ref=part.at[pl.ds(0, count)], dst_ref=res.at[pl.ds(0, count)],
            send_sem=res_send.at[0], recv_sem=res_recv.at[0],
            device_id=sibling, device_id_type=MESH)

    def sent(first, count, sem):
        rows = blk.at[pl.ds(first, count), core]
        return pltpu.make_async_remote_copy(
            src_ref=rows, dst_ref=rows, send_sem=sem, recv_sem=ici_recv.at[0, 0],
            device_id=sibling, device_id_type=MESH)

    def labels(slot, half):
        return blk[slot, half, HALF:HALF + TILE, :].astype(jnp.float32)[0:8, 0:HALF]

    def column_labels(slot):
        row = labels(slot, core)
        labc[slot] = jnp.concatenate([row] * 16, axis=0).T

    have_labc, have_racc, have_cacc = set(), set(), set()

    def prepare(slot):
        if slot not in have_labc:
            have_labc.add(slot)
            column_labels(slot)

    def masked(scores, own, row):
        count = scores.shape[0] // 8
        match = own.reshape(count, 8, 128) == row[None]
        return jnp.where(match, scores.reshape(count, 8, 128), jnp.float32(-2.0))

    def dot(lhs, rhs):
        return lax.dot_general(lhs, rhs, (((1,), (1,)), ((), ())), preferred_element_type=jnp.float32)

    def own_block(which):
        prepare(0)
        half = core if which == 0 else other
        scores = dot(blk[0, core, 0:HALF, :], blk[0, half, 0:HALF, :])
        row = labels(0, half)
        own = labc[0]
        best = racc[0] if 0 in have_racc else jnp.full((HALF, 128), -2.0, jnp.float32)
        for q in range(0, HALF, 128):
            t = masked(scores[:, q:q + 128], own, row[:, q:q + 128]).reshape(HALF, 128)
            if which == 0:
                i = lax.broadcasted_iota(jnp.int32, (HALF, 128), 0)
                j = lax.broadcasted_iota(jnp.int32, (HALF, 128), 1) + q
                t = jnp.where(i == j, jnp.float32(-2.0), t)
            best = jnp.maximum(best, t)
        racc[0] = best
        have_racc.add(0)

    def pairs(slot, others):
        prepare(slot)
        lhs = blk[slot, core, 0:HALF, :]
        own = labc[slot]
        best = racc[slot] if slot in have_racc else None
        for mate in others:
            scores = dot(lhs, blk[mate, :, 0:HALF, :].reshape(2 * HALF, WIDTH))
            for half in range(2):
                row = labels(mate, half)
                for q in range(0, HALF, 128):
                    at = half * HALF + q
                    t = masked(scores[:, at:at + 128], own, row[:, q:q + 128])
                    top = jnp.max(t, axis=0)
                    if mate in have_cacc:
                        top = jnp.maximum(top, cacc[mate, half, :, q:q + 128])
                    cacc[mate, half, :, q:q + 128] = top
                    t = t.reshape(HALF, 128)
                    best = t if best is None else jnp.maximum(best, t)
            have_cacc.add(mate)
        racc[slot] = best
        have_racc.add(slot)

    def finish(slot):
        if slot in have_racc:
            best = jnp.max(racc[slot].T.reshape(16, 8, HALF), axis=0)
            if slot in have_cacc:
                best = jnp.maximum(best, cacc[slot, core])
            part[2 * slot + core] = jnp.max(best, axis=0, keepdims=True)
        if slot in have_cacc:
            part[2 * slot + other] = jnp.max(cacc[slot, other], axis=0, keepdims=True)
            if slot not in have_racc:
                part[2 * slot + core] = jnp.max(cacc[slot, core], axis=0, keepdims=True)

    def send_back(slot):
        halves = (other,) if slot == 0 else (0, 1) if slot in have_cacc else (core,)
        for half in halves:
            result(slot, half, 1 if slot == 0 else core).start()

    finished = []
    for act in ACTS + (("",),):
        kind = act[0]
        if kind != "F":
            for slot in sorted(finished, key=hops, reverse=True):
                send_back(slot)
            finished = []
        if kind == "S":
            ici(act[1], act[2], act[3], act[4]).start()
        elif kind == "R":
            ici(act[1], act[1], act[2], 0).wait_recv()
        elif kind == "D":
            d2d(act[1], core).start()
        elif kind == "X":
            d2d(act[1], other).wait_recv()
        elif kind == "self":
            own_block(act[1])
        elif kind == "G":
            pairs(act[1], act[2])
        elif kind == "F":
            finish(act[1])
            finished.append(act[1])

    sent(1, SLOTS - 1, ici_send.at[0]).wait_send()
    sent(0, sum(act[0] == "D" for act in ACTS), d2d_send.at[0]).wait_send()
    count = 1 + sum(2 if slot in have_cacc else 1 for slot in range(1, SLOTS))
    results(count).wait_send()
    results(count).wait_recv()
    best = jnp.maximum(part[core], res[1])
    for slot in range(1, SLOTS):
        if slot in have_cacc:
            best = jnp.maximum(best, jnp.maximum(res[2 * slot], res[2 * slot + 1]))
        else:
            best = jnp.maximum(best, res[2 * slot + core])
    out_ref[...] = best.reshape(HALF)


def on_device(embeddings, destinations):
    nearest = pl.pallas_call(
        kernel,
        out_shape=jax.ShapeDtypeStruct((HALF,), jnp.float32),
        in_specs=[pl.BlockSpec(memory_space=pl.ANY)] * 2,
        out_specs=pl.BlockSpec(memory_space=pltpu.VMEM),
        scratch_shapes=[
            pltpu.VMEM((HALF, WIDTH), jnp.float32),
            pltpu.VMEM((1, HALF), jnp.int32),
            pltpu.SemaphoreType.DMA((2,)),
            pltpu.VMEM((SLOTS, 2, HALF + TILE, WIDTH), jnp.bfloat16),
            pltpu.VMEM((SLOTS, HALF, 128), jnp.float32),
            pltpu.VMEM((SLOTS, HALF, 128), jnp.float32),
            pltpu.VMEM((SLOTS, 2, 8, HALF), jnp.float32),
            pltpu.VMEM((2 * SLOTS, 1, HALF), jnp.float32),
            pltpu.VMEM((2 * SLOTS, 1, HALF), jnp.float32),
            pltpu.SemaphoreType.DMA((1,)),
            pltpu.SemaphoreType.DMA((SLOTS, len(PARTS))),
            pltpu.SemaphoreType.DMA((1,)),
            pltpu.SemaphoreType.DMA((SLOTS,)),
            pltpu.SemaphoreType.DMA((1,)),
            pltpu.SemaphoreType.DMA((1,)),
        ],
        compiler_params=pltpu.CompilerParams(
            collective_id=0, has_side_effects=True, vmem_limit_bytes=63 * 2**20),
    )(embeddings, destinations.reshape(1, HALF))
    return nearest


def solution(mesh):
    spec = P(("cluster", "group"), None)
    return jax.shard_map(
        on_device, mesh=mesh, in_specs=(spec, spec), out_specs=P(("cluster", "group")), check_vma=False
    )
```
